32 devices in a mesh: rep: 2 (over y), pool: 16 (over z, x, core).
Axes of the slice: x: 2, y: 2, z: 4, core: 2. Of those that a mesh axis runs over, the one named last changes fastest.
Arguments:
- tokens: bfloat16 [4096, 8192], P(('rep', 'pool')), parts along dimension 0, may hold values from -6 to 6
- key_projection_weight: bfloat16 [8192, 1024], P('pool'), may hold values from -0.0625 to 0.0625
- adapter_down_factors: bfloat16 [32, 8192, 64], P(('rep', 'pool')), parts along dimension 0, may hold values from -0.0625 to 0.0625
- adapter_up_factors: bfloat16 [32, 64, 1024], P(('rep', 'pool')), parts along dimension 0, may hold values from -0.75 to 0.75
- request_adapter_index: int32 [4096, 1], P(('rep', 'pool')), parts along dimension 0, may hold values from 0 to 15; in each aligned block of 128 rows (0 to 127, 128 to 255, ...) at most 16 rows name the same one
Outputs:
- queries: bfloat16 [4096, 1024], P(('rep', 'pool')), parts along dimension 0
The draws below stay inside these ranges and needn't reach their ends.
There are 2 independent parts, one for each index of `rep`. The reference program is written for one: setup_inputs(seed, part) draws one part's arguments, and reference() takes and returns one part's arrays. A program takes and returns all parts, laid end to end along the dimension named above; an argument that names none is the same for every part. Nothing has to cross between parts.
Inputs may be any that keep to these rules, and one draw needn't show every extreme that they name: `request_adapter_index`: in each aligned block of 128 rows (the rows of one index of pool) no adapter is named by more than 16 rows, a bound that some block reaches.
All inputs are finite; a program needn't handle non-finite values.
Results may differ from the reference program's by a relative error of at most 0.0055.
Values may be sent and summed in bfloat16 or wider, within the bound.
A program may use at most 128 MiB of HBM per device.

```python
import math
import jax
import jax.numpy as jnp
import numpy as np
from jax import lax

MODEL_WIDTH = 8192
KEY_OUT_WIDTH = 1024
ADAPTER_RANK = 64
TOK_DEV = 128
ADAPTER_COUNT = 16
MOST = 16
TOKENS = 2048
N_POOL = 16


def level_of(rng, shape, pieces, smallest, high):
    gain, own = 1.0, jax.random.fold_in(rng, 6)
    for axis_at, blocks in pieces:
        steps = jnp.exp(jax.random.uniform(jax.random.fold_in(own, axis_at), (blocks,), jnp.float32, smallest / len(pieces), high / len(pieces)))
        gain = gain * jnp.repeat(steps, shape[axis_at] // blocks).reshape([-1 if axis == axis_at else 1 for axis in range(len(shape))])
    return gain


def routed_block(own_key, own, number, rows, amount, top, bound, lean):
    order = jax.random.permutation(own_key, amount)
    heavy_load, common = load_shares(amount, rows * top, bound, lean, True), load_shares(amount, rows * top, bound, lean, False)
    places = jnp.arange(amount)

    def named(lengths, rotation):
        used = int((lengths > 0).sum())
        fixed = max(1, used // 4)
        moved = fixed + (places - fixed + rotation * (used - fixed)) % max(1, amount - fixed)
        return jnp.zeros((amount,), jnp.int32).at[order[jnp.where(places < fixed, places, moved)]].set(jnp.asarray(lengths, jnp.int32))

    lengths = jnp.where(number % 4 == 0, named(heavy_load, number // 4), named(common, number - number // 4 - 1))
    mixed = jax.random.permutation(jax.random.fold_in(own, 3), amount)
    giver, sink = mixed[0:amount // 2 * 2:2], mixed[1:amount // 2 * 2:2]
    room = jnp.minimum(lengths[giver] - 1, bound - lengths[sink]) // 2
    room = jnp.where((giver == order[0]) | (sink == order[0]) | (lengths[sink] == 0), 0, jnp.maximum(room, 0))
    moved = jax.random.randint(jax.random.fold_in(own, 4), (amount // 2,), 0, 1 << 20) % (room + 1)
    lengths = lengths.at[giver].add(-moved).at[sink].add(moved)
    labels = jnp.searchsorted(jnp.cumsum(lengths), jnp.arange(rows * top), side="right").astype(jnp.int32)
    grid = labels.reshape(top, rows).T
    grid = grid[jax.random.permutation(jax.random.fold_in(own, 1), rows)]
    rotation = jax.random.randint(jax.random.fold_in(own, 2), (rows, 1), 0, top)
    return jnp.take_along_axis(grid, (jnp.arange(top)[None, :] + rotation) % top, axis=1)


def load_shares(amount, total, most, lean, full):
    weights = [(1 << 20) // math.isqrt(standing ** lean) + 1 for standing in range(1, amount + 1)]
    largest = most if full else min(most, max(-(-total // amount), total * weights[0] // sum(weights)))
    least = 1 if total - largest >= amount - 1 else 0
    counts, rest = [largest] + [least] * (amount - 1), total - largest - least * (amount - 1)
    while rest > 0:
        free = [i for i in range(1, amount) if counts[i] < largest] or [i for i in range(1, amount) if counts[i] < most]
        mass, budget = sum([weights[i] for i in free]), rest
        for i in free:
            extra = min(most - counts[i], max(1, budget * weights[i] // mass), rest)
            counts[i] = counts[i] + extra
            rest = rest - extra
    return np.array(counts)


def normal_values(key, extent, width, reach, pieces=(), kind=jnp.bfloat16):
    drawn = width * jax.random.normal(key, extent, jnp.float32)
    if pieces:
        drawn = drawn * level_of(key, extent, pieces, -0.22, 0.18)
    return jnp.clip(drawn, -reach, reach).astype(kind)


def setup_inputs(seed: int = 0, part: int = 0) -> dict:
    key_of = jax.random.split(jax.random.key(seed), 6)
    part_splits = jax.random.split(jax.random.fold_in(key_of[5], part), 6)
    tokens = normal_values(part_splits[0], (TOKENS, MODEL_WIDTH), 1.0, 6.0, ((0, 16),))
    key_projection_weight = normal_values(key_of[1], (MODEL_WIDTH, KEY_OUT_WIDTH), MODEL_WIDTH ** -0.5, 0.0625, ((0, 16),))
    adapter_down_factors = normal_values(part_splits[2], (ADAPTER_COUNT, MODEL_WIDTH, ADAPTER_RANK), MODEL_WIDTH ** -0.5, 0.0625, ((0, 16),))
    adapter_up_factors = normal_values(part_splits[3], (ADAPTER_COUNT, ADAPTER_RANK, KEY_OUT_WIDTH), ADAPTER_RANK ** -0.5, 0.75, ((0, 16),))
    request_adapter_index_keys = jax.random.split(jax.random.fold_in(part_splits[4], 1), TOKENS // TOK_DEV)
    request_adapter_index_turns = jax.random.permutation(jax.random.fold_in(part_splits[4], 3), TOKENS // TOK_DEV)
    request_adapter_index = jax.vmap(lambda own, number: routed_block(jax.random.fold_in(part_splits[4], 2), own, number, TOK_DEV, ADAPTER_COUNT, 1, MOST, 2))(request_adapter_index_keys, request_adapter_index_turns).reshape((TOKENS, 1))
    return dict(tokens=tokens, key_projection_weight=key_projection_weight, adapter_down_factors=adapter_down_factors, adapter_up_factors=adapter_up_factors, request_adapter_index=request_adapter_index)


def one_source(block_tokens, block_ids, gathered_down_factors, gathered_up_factors):
    same = block_ids[:, None] == block_ids[None, :]
    positions = jnp.arange(block_ids.shape[0], dtype=jnp.int32)
    earlier = positions[None, :] < positions[:, None]
    rank_within = jnp.sum((same & earlier).astype(jnp.int32), axis=1).astype(jnp.int32)
    slot_index = (block_ids * MOST + rank_within).astype(jnp.int32)
    slots = jnp.zeros((ADAPTER_COUNT * MOST, MODEL_WIDTH), jnp.float32).at[slot_index].set(block_tokens.astype(jnp.float32))
    slots = slots.reshape(ADAPTER_COUNT, MOST, MODEL_WIDTH)
    rank_reduced = jnp.einsum("amd,adr->amr", slots, gathered_down_factors).astype(jnp.bfloat16)
    expanded = jnp.einsum("amr,are->ame", rank_reduced.astype(jnp.float32), gathered_up_factors).astype(jnp.bfloat16)
    return expanded.reshape(ADAPTER_COUNT * MOST, KEY_OUT_WIDTH)[slot_index]


def reference(tokens, key_projection_weight, adapter_down_factors, adapter_up_factors, request_adapter_index):
    base = jnp.dot(tokens, key_projection_weight, preferred_element_type=jnp.float32)
    gathered_down_factors = adapter_down_factors.astype(jnp.float32)
    gathered_up_factors = adapter_up_factors.astype(jnp.float32)
    blocks = tokens.reshape(N_POOL, TOK_DEV, MODEL_WIDTH)
    block_ids = request_adapter_index[:, 0].astype(jnp.int32).reshape(N_POOL, TOK_DEV)
    expanded = lax.map(lambda pair: one_source(pair[0], pair[1], gathered_down_factors, gathered_up_factors), (blocks, block_ids))
    expanded = expanded.reshape(TOKENS, KEY_OUT_WIDTH)
    return (base + 2.0 * expanded.astype(jnp.float32)).astype(jnp.bfloat16)
```

```python
import functools

import jax
import jax.numpy as jnp
from jax import lax
from jax.experimental import pallas as pl
from jax.experimental.pallas import tpu as pltpu
from jax.sharding import PartitionSpec as P

HALVES = 2
LANES = 128
MESH = pl.DeviceIdType.MESH


def kernel(
    group, reps, parts,
    x_hbm, w_hbm, a_ref, b_hbm, id_ref, out_ref,
    apack, xr, ar, wf, bp, idr, idb, acc0, acc1, sp, srecv, s2, s2m, cpart, crecv,
    x_send, x_recv, a_send, a_recv, w_send, w_recv, f_send, f_recv, b_send, b_recv,
    i_send, i_recv, s_send, s_recv, t_send, t_recv, c_send, c_recv, local_sem,
):
    rep = lax.axis_index("rep")
    pool = lax.axis_index("pool")
    half, e = pool // group, pool % group
    rows, out_width = out_ref.shape
    depth = w_hbm.shape[0]
    low = group * depth
    rank = b_hbm.shape[0]
    devices = group * HALVES
    part = out_width // parts
    partner = (pool + group) % devices

    def peer(k):
        return half * group + (e + k) % group

    def row_at(i):
        return pl.ds(pl.multiple_of(i * rows, rows), rows)

    def col_at(i, size):
        return pl.ds(pl.multiple_of(i * size, size), size)

    def remote(src, dst, send, recv, device):
        return pltpu.make_async_remote_copy(
            src_ref=src, dst_ref=dst, send_sem=send, recv_sem=recv,
            device_id=device, device_id_type=MESH,
        )

    barrier = pltpu.get_barrier_semaphore()
    for k in range(1, devices):
        pl.semaphore_signal(
            barrier, inc=1, device_id={"pool": (pool + k) % devices}, device_id_type=MESH
        )
    for k in range(1, reps):
        pl.semaphore_signal(
            barrier, inc=1, device_id={"rep": (rep + k) % reps}, device_id_type=MESH
        )

    own = [
        pltpu.make_async_copy(
            x_hbm.at[:, pl.ds(pl.multiple_of(b * low + e * depth, depth), depth)],
            xr.at[b, row_at(e)], local_sem.at[b],
        )
        for b in range(HALVES)
    ]
    own.append(pltpu.make_async_copy(w_hbm, wf.at[half], local_sem.at[2]))
    own_b = pl.ds(pl.multiple_of(half * rank, rank), rank)
    own.append(pltpu.make_async_copy(b_hbm, bp.at[own_b], local_sem.at[3]))
    for copy in own:
        copy.start()

    @pl.loop(0, group)
    def _(i):
        at = pl.ds(pl.multiple_of(i * depth, depth), depth)
        up = pl.ds(pl.multiple_of(low + i * depth, depth), depth)
        apack[at] = jnp.concatenate([a_ref[at], a_ref[up]], axis=1)

    ar[:, col_at(pool, LANES)] = apack[pl.ds(pl.multiple_of(e * depth, depth), depth)]
    idr[e] = id_ref[...]
    pl.semaphore_wait(barrier, devices - 1 + reps - 1)

    sends, arrivals = [], []

    def launch(copy, wanted=True):
        copy.start()
        sends.append(copy)
        if wanted:
            arrivals.append(copy)
        return copy

    def send_a(n, device):
        to = device % group
        launch(remote(
            apack.at[pl.ds(pl.multiple_of(to * depth, depth), depth)],
            ar.at[:, col_at(pool, LANES)], a_send.at[n], a_recv.at[n], {"pool": device},
        ))

    for k in range(1, group):
        launch(remote(id_ref, idr.at[e], i_send.at[k], i_recv.at[k], {"pool": peer(k)}))
    for k in range(1, group):
        for b in range(HALVES):
            to = (e + k) % group
            launch(remote(
                x_hbm.at[:, pl.ds(pl.multiple_of(b * low + to * depth, depth), depth)],
                xr.at[b, row_at(e)], x_send.at[b, k], x_recv.at[b, k], {"pool": peer(k)},
            ))
        send_a(k, peer(k))
        send_a(group + k, (1 - half) * group + (e + k) % group)
    send_a(group, partner)
    share = parts // reps
    w_copies = []
    for n in range(share):
        at = col_at(n * reps + rep, part)
        w_copies.append(launch(remote(
            w_hbm.at[:, at], wf.at[half, :, at], w_send.at[n], w_recv.at[n], {"pool": partner},
        ), False))
    b_copy = launch(remote(b_hbm, bp.at[own_b], b_send, b_recv, {"pool": partner}), False)

    for copy in arrivals:
        copy.wait_recv()
    for copy in own:
        copy.wait()

    lane = lax.broadcasted_iota(jnp.int32, (rows, LANES), 1)
    eye = lane == lax.broadcasted_iota(jnp.int32, (rows, LANES), 0)

    @pl.loop(0, group)
    def _(i):
        line = jnp.broadcast_to(idr[i][0:1, :], (rows, LANES))
        column = jnp.sum(jnp.where(eye, line, 0.0), axis=1, keepdims=True)
        idb[row_at(i)] = jnp.broadcast_to(column, (rows, LANES))

    acc0[...] = jnp.zeros_like(acc0)
    acc1[...] = jnp.zeros_like(acc1)

    @pl.loop(0, devices // 2)
    def _(j):
        at = col_at(j, 2 * LANES)
        ids = idb[...]
        first = (2 * j).astype(jnp.float32)
        for b, acc in ((0, acc0), (1, acc1)):
            t = jnp.dot(xr[b], ar[:, at], preferred_element_type=jnp.float32)
            acc[...] = jnp.where(
                ids == first, t[:, :LANES],
                jnp.where(ids == first + 1.0, t[:, LANES:], acc[...]),
            )

    wide = lax.broadcasted_iota(jnp.int32, acc0.shape, 1)
    sp[...] = jnp.where(wide < rank, acc0[...], acc1[...]).astype(jnp.bfloat16)
    s_copies = []
    for k in range(1, group):
        to = (e + k) % group
        s_copies.append(launch(remote(
            sp.at[row_at(to)], srecv.at[k], s_send.at[k], s_recv.at[k], {"pool": peer(k)},
        ), False))
    other = (rep + 1) % reps
    f_copies = []
    for n in range(share):
        w_copies[n].wait_recv()
        at = col_at(n * reps + rep, part)
        piece = wf.at[1 - half, :, at]
        f_copies.append(launch(remote(
            piece, piece, f_send.at[n], f_recv.at[n], {"rep": other},
        ), False))
    total = sp[row_at(e)].astype(jnp.float32)
    for k in range(1, group):
        s_copies[k - 1].wait_recv()
        total += srecv[k].astype(jnp.float32)
    total = total + pltpu.roll(total, rank, 1)
    upper = idb[row_at(e)] >= float(group)
    s2[row_at(e)] = jnp.where(upper == (lane >= rank), total, 0.0).astype(jnp.bfloat16)
    t_copies = []
    for k in range(1, group):
        t_copies.append(launch(remote(
            s2.at[row_at(e)], s2.at[row_at(e)], t_send.at[k], t_recv.at[k], {"pool": peer(k)},
        ), False))
    for copy in t_copies:
        copy.wait_recv()
    b_copy.wait_recv()
    mine = e.astype(jnp.float32)
    ids = idb[...]
    here = (ids == mine) | (ids == mine + float(group))
    s2m[...] = jnp.where(here, 2.0 * s2[...].astype(jnp.float32), 0.0).astype(jnp.bfloat16)

    for copy in f_copies:
        copy.wait_recv()
    c_copies = []
    for j in range(parts):
        at = pl.ds(j * part, part)
        value = jnp.dot(s2m[...], bp[:, at], preferred_element_type=jnp.float32)
        for b in range(HALVES):
            value += jnp.dot(xr[b], wf[b, :, at], preferred_element_type=jnp.float32)
        cpart[:, at] = value.astype(jnp.bfloat16)
        for k in range(1, group):
            to = (e + k) % group
            c_copies.append(launch(remote(
                cpart.at[row_at(to), at], crecv.at[k, :, at],
                c_send.at[j, k], c_recv.at[j, k], {"pool": peer(k)},
            ), False))
    for j in range(parts):
        at = pl.ds(j * part, part)
        value = cpart[row_at(e), at].astype(jnp.float32)
        for k in range(1, group):
            c_copies[j * (group - 1) + k - 1].wait_recv()
            value += crecv[k, :, at].astype(jnp.float32)
        out_ref[:, at] = value.astype(jnp.bfloat16)
    for copy in sends:
        copy.wait_send()


def split_depth(
    tokens, key_projection_weight, adapter_down_factors, adapter_up_factors, request_adapter_index
):
    rows = tokens.shape[0]
    depth, out_width = key_projection_weight.shape
    rank = adapter_down_factors.shape[2]
    devices = lax.axis_size("pool")
    reps = lax.axis_size("rep")
    group = devices // HALVES
    parts = 2 * reps
    everyone = group * rows
    ids = jnp.broadcast_to(
        request_adapter_index.astype(jnp.float32).reshape(1, rows), (8, rows)
    )
    bf16, f32 = jnp.bfloat16, jnp.float32
    dma = pltpu.SemaphoreType.DMA
    hbm, vmem = pl.BlockSpec(memory_space=pl.ANY), pl.BlockSpec(memory_space=pltpu.VMEM)
    return pl.pallas_call(
        functools.partial(kernel, group, reps, parts),
        out_shape=jax.ShapeDtypeStruct((rows, out_width), bf16),
        in_specs=[hbm, hbm, vmem, hbm, vmem],
        out_specs=vmem,
        scratch_shapes=[
            pltpu.VMEM((group * depth, LANES), bf16),
            pltpu.VMEM((HALVES, everyone, depth), bf16),
            pltpu.VMEM((depth, devices * LANES), bf16),
            pltpu.VMEM((HALVES, depth, out_width), bf16),
            pltpu.VMEM((HALVES * rank, out_width), bf16),
            pltpu.VMEM((group, 8, rows), f32),
            pltpu.VMEM((everyone, LANES), f32),
            pltpu.VMEM((everyone, LANES), f32),
            pltpu.VMEM((everyone, LANES), f32),
            pltpu.VMEM((everyone, LANES), bf16),
            pltpu.VMEM((group, rows, LANES), bf16),
            pltpu.VMEM((everyone, LANES), bf16),
            pltpu.VMEM((everyone, LANES), bf16),
            pltpu.VMEM((everyone, out_width), bf16),
            pltpu.VMEM((group, rows, out_width), bf16),
            dma((HALVES, group)), dma((HALVES, group)),
            dma((devices,)), dma((devices,)),
            dma((parts,)), dma((parts,)),
            dma((parts,)), dma((parts,)),
            dma, dma,
            dma((group,)), dma((group,)),
            dma((group,)), dma((group,)),
            dma((group,)), dma((group,)),
            dma((parts, group)), dma((parts, group)),
            dma((4,)),
        ],
        compiler_params=pltpu.CompilerParams(
            collective_id=0, has_side_effects=True, vmem_limit_bytes=48 << 20
        ),
    )(
        tokens, key_projection_weight, adapter_down_factors[0], adapter_up_factors[0], ids
    )


def route_rows(
    tokens, key_projection_weight, adapter_down_factors, adapter_up_factors, request_adapter_index
):
    row_count = tokens.shape[0]
    width = tokens.shape[1]
    devices = lax.axis_size("pool")
    rows_by_device = adapter_down_factors.shape[0]
    out_width = key_projection_weight.shape[1]
    per_adapter = max(2, 2 * row_count // (rows_by_device * devices))
    capacity = rows_by_device * per_adapter
    adapter_col = request_adapter_index[:, 0]
    same = adapter_col[:, None] == adapter_col[None, :]
    positions = jnp.arange(row_count, dtype=jnp.int32)
    earlier = positions[None, :] < positions[:, None]
    rank_within = jnp.sum((same & earlier).astype(jnp.int32), axis=1)
    slot_index = adapter_col * per_adapter + rank_within
    base = jnp.dot(
        tokens,
        lax.all_gather(key_projection_weight, "pool", axis=0, tiled=True),
        preferred_element_type=jnp.float32,
    )
    outgoing = jnp.zeros((devices * capacity, width), jnp.bfloat16).at[slot_index].set(tokens)
    outgoing = outgoing.reshape(devices, capacity, width)
    received_rows = lax.all_to_all(outgoing, "pool", split_axis=0, concat_axis=0, tiled=True)
    received_rows = received_rows.reshape(devices, rows_by_device, per_adapter, width)
    rank_reduced = jnp.einsum(
        "qhey,hyt->qhet", received_rows, adapter_down_factors, preferred_element_type=jnp.float32
    ).astype(jnp.bfloat16)
    expanded = jnp.einsum(
        "zydk,ykj->zydj", rank_reduced, adapter_up_factors, preferred_element_type=jnp.float32
    ).astype(jnp.bfloat16)
    returned = lax.all_to_all(
        expanded.reshape(devices, capacity, out_width),
        "pool",
        split_axis=0,
        concat_axis=0,
        tiled=True,
    )
    delta = returned.reshape(devices * capacity, out_width)[slot_index]
    return (base + 2.0 * delta.astype(jnp.float32)).astype(jnp.bfloat16)


def local(
    tokens, key_projection_weight, adapter_down_factors, adapter_up_factors, request_adapter_index
):
    fits = (
        key_projection_weight.shape[0] % LANES == 0
        and tokens.shape[0] == LANES
        and adapter_down_factors.shape[0] == 1
        and HALVES * adapter_down_factors.shape[2] == LANES
        and lax.axis_size("pool") % HALVES == 0
        and lax.axis_size("rep") == 2
    )
    plan = split_depth if fits else route_rows
    return plan(
        tokens, key_projection_weight, adapter_down_factors, adapter_up_factors,
        request_adapter_index,
    )


def solution(mesh):
    in_specs = (
        P(("rep", "pool"), None),
        P("pool", None),
        P(("rep", "pool"), None, None),
        P(("rep", "pool"), None, None),
        P(("rep", "pool"), None),
    )
    out_specs = P(("rep", "pool"), None)
    return jax.shard_map(local, mesh=mesh, in_specs=in_specs, out_specs=out_specs, check_vma=False)
```

```python
import functools

import jax
import jax.numpy as jnp
from jax import lax
from jax.experimental import pallas as pl
from jax.experimental.pallas import tpu as pltpu
from jax.sharding import PartitionSpec as P

HALVES = 2
CORES = 2
W_FIRST = False
LANES = 128
MESH = pl.DeviceIdType.MESH


def kernel(
    group, reps, parts,
    x_hbm, w_hbm, a_hbm, b_hbm, id_ref, out_ref,
    xr, ar, wf, bp, idr, slots, acc, base, srecv, s2, s2m, cpart, pair, cpair, crecv,
    x_send, x_recv, a_send, a_recv, w_send, w_recv, f_send, f_recv, b_send, b_recv,
    i_send, i_recv, s_send, s_recv, t_send, t_recv, p_send, p_recv, c_send, c_recv, local_sem,
):
    rep = lax.axis_index("rep")
    pool = lax.axis_index("pool")
    half, e = pool // group, pool % group
    rows, out_width = out_ref.shape
    depth = w_hbm.shape[0]
    low = group * depth
    rank = b_hbm.shape[0]
    devices = group * HALVES
    part = out_width // parts
    partner = (pool + group) % devices
    sides = group // CORES
    core = e % CORES
    core_peer = half * group + e + 1 - 2 * core

    def peer(k):
        return half * group + (e + k) % group

    def place(i):
        return (i % CORES) * sides + i // CORES

    def row_at(i, count=1):
        return pl.ds(pl.multiple_of(i * rows, rows), count * rows)

    def col_at(i, size):
        return pl.ds(pl.multiple_of(i * size, size), size)

    def depth_at(b, i):
        return pl.ds(pl.multiple_of(b * low + i * depth, depth), depth)

    def remote(src, dst, send, recv, device):
        return pltpu.make_async_remote_copy(
            src_ref=src, dst_ref=dst, send_sem=send, recv_sem=recv,
            device_id=device, device_id_type=MESH,
        )

    barrier = pltpu.get_barrier_semaphore()
    for k in range(1, devices):
        pl.semaphore_signal(
            barrier, inc=1, device_id={"pool": (pool + k) % devices}, device_id_type=MESH
        )
    for k in range(1, reps):
        pl.semaphore_signal(
            barrier, inc=1, device_id={"rep": (rep + k) % reps}, device_id_type=MESH
        )

    my_place = place(e)
    my_rows = row_at(my_place)
    slot = e * HALVES + half
    my_slot = pl.ds(pl.multiple_of(slot * rank, rank), rank)
    own_b = pl.ds(pl.multiple_of(half * rank, rank), rank)
    own = [
        pltpu.make_async_copy(w_hbm, wf.at[half], local_sem.at[0]),
        pltpu.make_async_copy(b_hbm, bp.at[own_b], local_sem.at[1]),
    ]
    for b in range(HALVES):
        own.append(pltpu.make_async_copy(
            x_hbm.at[:, depth_at(b, e)], xr.at[b, my_rows], local_sem.at[2 + 2 * b]
        ))
        own.append(pltpu.make_async_copy(
            a_hbm.at[:, depth_at(b, e)], ar.at[b, my_slot], local_sem.at[3 + 2 * b]
        ))
    for copy in own:
        copy.start()
    idr[my_place] = id_ref[...]
    pl.semaphore_wait(barrier, devices - 1 + reps - 1)

    sends, x_copies, a_copies = [], [], []

    def launch(copy):
        copy.start()
        sends.append(copy)
        return copy

    def send_a(n, device):
        for b in range(HALVES):
            a_copies.append(launch(remote(
                a_hbm.at[:, depth_at(b, device % group)], ar.at[b, my_slot],
                a_send.at[b, n], a_recv.at[b, n], {"pool": device},
            )))

    share = parts // reps
    w_copies = []

    def send_w():
        for n in range(share):
            at = col_at(n * reps + rep, part)
            w_copies.append(launch(remote(
                w_hbm.at[:, at], wf.at[half, :, at], w_send.at[n], w_recv.at[n],
                {"pool": partner},
            )))

    if W_FIRST:
        send_w()
    for k in range(1, group):
        x_copies.append(launch(remote(
            id_ref, idr.at[my_place], i_send.at[k], i_recv.at[k], {"pool": peer(k)}
        )))
    for k in range(1, group):
        for b in range(HALVES):
            x_copies.append(launch(remote(
                x_hbm.at[:, depth_at(b, (e + k) % group)], xr.at[b, my_rows],
                x_send.at[b, k], x_recv.at[b, k], {"pool": peer(k)},
            )))
        send_a(group + k, (1 - half) * group + (e + k) % group)
        send_a(k, peer(k))
    send_a(group, partner)
    if not W_FIRST:
        send_w()
    b_copy = launch(remote(b_hbm, bp.at[own_b], b_send, b_recv, {"pool": partner}))

    for copy in x_copies:
        copy.wait_recv()
    for copy in own:
        copy.wait()

    lane = lax.broadcasted_iota(jnp.int32, (rows, LANES), 1)
    eye = lane == lax.broadcasted_iota(jnp.int32, (rows, LANES), 0)
    upper = jnp.where(lane >= rank, 1.0, 0.0)

    @pl.loop(0, group)
    def _(i):
        line = jnp.broadcast_to(idr[i], (rows, LANES)).astype(jnp.float32)
        column = jnp.sum(jnp.where(eye, line, 0.0), axis=1, keepdims=True)
        column = jnp.where(
            column >= float(group), HALVES * (column - float(group)) + 1.0, HALVES * column
        )
        slots[row_at(i)] = jnp.broadcast_to(column, (rows, LANES)) - upper

    @pl.loop(0, parts)
    def _(j):
        at = col_at(j, part)
        base[:, at] = jnp.dot(
            xr[half], wf[half, :, at], preferred_element_type=jnp.float32
        )

    def forward_w():
        copies = []
        for n in range(share):
            w_copies[n].wait_recv()
            piece = wf.at[1 - half, :, col_at(n * reps + rep, part)]
            copies.append(launch(remote(
                piece, piece, f_send.at[n], f_recv.at[n], {"rep": (rep + 1) % reps}
            )))
        return copies

    if W_FIRST:
        f_copies = forward_w()
    for copy in a_copies:
        copy.wait_recv()
    acc[...] = jnp.zeros_like(acc)
    wide = 4 * rank

    @pl.loop(0, devices * rank // wide)
    def _(j):
        at = pl.ds(pl.multiple_of(j * wide, wide), wide)
        t = jnp.zeros((group * rows, wide), jnp.float32)
        for b in range(HALVES):
            t += lax.dot_general(
                xr[b], ar[b, at], (((1,), (1,)), ((), ())),
                preferred_element_type=jnp.float32,
            )
        first = (4 * j).astype(jnp.float32)
        acc[...] = jnp.where(
            slots[...] == first, t[:, :LANES],
            jnp.where(slots[...] == first + 2.0, t[:, LANES:], acc[...]),
        )

    s_copies = []
    for k in range(1, group):
        s_copies.append(launch(remote(
            acc.at[row_at(place((e + k) % group))], srecv.at[k], s_send.at[k], s_recv.at[k],
            {"pool": peer(k)},
        )))
    if not W_FIRST:
        f_copies = forward_w()
    total = acc[my_rows]
    for k in range(1, group):
        s_copies[k - 1].wait_recv()
        total += srecv[k]
    s2[my_rows] = total.astype(jnp.bfloat16)
    t_copies = []
    for k in range(1, group):
        t_copies.append(launch(remote(
            s2.at[my_rows], s2.at[my_rows], t_send.at[k], t_recv.at[k], {"pool": peer(k)}
        )))

    for n in range(share):
        f_copies[n].wait_recv()

    @pl.loop(0, parts)
    def _(j):
        at = col_at(j, part)
        base[:, at] += jnp.dot(
            xr[1 - half], wf[1 - half, :, at], preferred_element_type=jnp.float32
        )

    for copy in t_copies:
        copy.wait_recv()
    b_copy.wait_recv()
    mine = (HALVES * e).astype(jnp.float32)
    s2m[...] = jnp.where(
        slots[...] == mine, s2[...].astype(jnp.float32), 0.0
    ).astype(jnp.bfloat16)

    here, there = row_at(core * sides, sides), row_at((1 - core) * sides, sides)
    p_copies, c_copies = [], []

    def pair_up(j):
        at = pl.ds(j * part, part)
        update = jnp.dot(s2m[...], bp[:, at], preferred_element_type=jnp.float32)
        update = update.astype(jnp.bfloat16).astype(jnp.float32)
        base[:, at] += 2.0 * update
        cpart[:, at] = base[there, at].astype(jnp.bfloat16)
        p_copies.append(launch(remote(
            cpart.at[:, at], pair.at[:, at], p_send.at[j], p_recv.at[j], {"pool": core_peer}
        )))

    def hand_on(j):
        at = pl.ds(j * part, part)
        p_copies[j].wait_recv()
        cpair[:, at] = (base[here, at] + pair[:, at].astype(jnp.float32)).astype(jnp.bfloat16)
        for k in range(1, sides):
            to = (e // CORES + k) % sides
            c_copies.append(launch(remote(
                cpair.at[row_at(to), at], crecv.at[k, :, at], c_send.at[j, k], c_recv.at[j, k],
                {"pool": half * group + to * CORES + core},
            )))

    for j in range(parts):
        pair_up(j)
        if j > 0:
            hand_on(j - 1)
    hand_on(parts - 1)
    for j in range(parts):
        at = pl.ds(j * part, part)
        value = cpair[row_at(e // CORES), at].astype(jnp.float32)
        for k in range(1, sides):
            c_copies[j * (sides - 1) + k - 1].wait_recv()
            value += crecv[k, :, at].astype(jnp.float32)
        out_ref[:, at] = value.astype(jnp.bfloat16)
    for copy in sends:
        copy.wait_send()


def split_depth(
    tokens, key_projection_weight, adapter_down_factors, adapter_up_factors, request_adapter_index
):
    rows = tokens.shape[0]
    depth, out_width = key_projection_weight.shape
    rank = adapter_down_factors.shape[2]
    devices = lax.axis_size("pool")
    reps = lax.axis_size("rep")
    group = devices // HALVES
    sides = group // CORES
    parts = 2 * reps
    everyone = group * rows
    ids = request_adapter_index.reshape(1, rows)
    bf16, f32 = jnp.bfloat16, jnp.float32
    dma = pltpu.SemaphoreType.DMA
    hbm, vmem = pl.BlockSpec(memory_space=pl.ANY), pl.BlockSpec(memory_space=pltpu.VMEM)
    return pl.pallas_call(
        functools.partial(kernel, group, reps, parts),
        out_shape=jax.ShapeDtypeStruct((rows, out_width), bf16),
        in_specs=[hbm, hbm, hbm, hbm, vmem],
        out_specs=vmem,
        scratch_shapes=[
            pltpu.VMEM((HALVES, everyone, depth), bf16),
            pltpu.VMEM((HALVES, devices * rank, depth), bf16),
            pltpu.VMEM((HALVES, depth, out_width), bf16),
            pltpu.VMEM((HALVES * rank, out_width), bf16),
            pltpu.VMEM((group, 1, rows), jnp.int32),
            pltpu.VMEM((everyone, LANES), f32),
            pltpu.VMEM((everyone, LANES), f32),
            pltpu.VMEM((everyone, out_width), f32),
            pltpu.VMEM((group, rows, LANES), f32),
            pltpu.VMEM((everyone, LANES), bf16),
            pltpu.VMEM((everyone, LANES), bf16),
            pltpu.VMEM((sides * rows, out_width), bf16),
            pltpu.VMEM((sides * rows, out_width), bf16),
            pltpu.VMEM((sides * rows, out_width), bf16),
            pltpu.VMEM((sides, rows, out_width), bf16),
            dma((HALVES, group)), dma((HALVES, group)),
            dma((HALVES, devices)), dma((HALVES, devices)),
            dma((parts,)), dma((parts,)),
            dma((parts,)), dma((parts,)),
            dma, dma,
            dma((group,)), dma((group,)),
            dma((group,)), dma((group,)),
            dma((group,)), dma((group,)),
            dma((parts,)), dma((parts,)),
            dma((parts, sides)), dma((parts, sides)),
            dma((6,)),
        ],
        compiler_params=pltpu.CompilerParams(
            collective_id=0, has_side_effects=True, vmem_limit_bytes=60 << 20
        ),
    )(
        tokens, key_projection_weight, jnp.swapaxes(adapter_down_factors, 1, 2)[0],
        adapter_up_factors[0], ids,
    )


def route_rows(
    tokens, key_projection_weight, adapter_down_factors, adapter_up_factors, request_adapter_index
):
    row_count = tokens.shape[0]
    width = tokens.shape[1]
    devices = lax.axis_size("pool")
    rows_by_device = adapter_down_factors.shape[0]
    out_width = key_projection_weight.shape[1]
    per_adapter = max(2, 2 * row_count // (rows_by_device * devices))
    capacity = rows_by_device * per_adapter
    adapter_col = request_adapter_index[:, 0]
    same = adapter_col[:, None] == adapter_col[None, :]
    positions = jnp.arange(row_count, dtype=jnp.int32)
    earlier = positions[None, :] < positions[:, None]
    rank_within = jnp.sum((same & earlier).astype(jnp.int32), axis=1)
    slot_index = adapter_col * per_adapter + rank_within
    base = jnp.dot(
        tokens,
        lax.all_gather(key_projection_weight, "pool", axis=0, tiled=True),
        preferred_element_type=jnp.float32,
    )
    outgoing = jnp.zeros((devices * capacity, width), jnp.bfloat16).at[slot_index].set(tokens)
    outgoing = outgoing.reshape(devices, capacity, width)
    received_rows = lax.all_to_all(outgoing, "pool", split_axis=0, concat_axis=0, tiled=True)
    received_rows = received_rows.reshape(devices, rows_by_device, per_adapter, width)
    rank_reduced = jnp.einsum(
        "qhey,hyt->qhet", received_rows, adapter_down_factors, preferred_element_type=jnp.float32
    ).astype(jnp.bfloat16)
    expanded = jnp.einsum(
        "zydk,ykj->zydj", rank_reduced, adapter_up_factors, preferred_element_type=jnp.float32
    ).astype(jnp.bfloat16)
    returned = lax.all_to_all(
        expanded.reshape(devices, capacity, out_width),
        "pool",
        split_axis=0,
        concat_axis=0,
        tiled=True,
    )
    delta = returned.reshape(devices * capacity, out_width)[slot_index]
    return (base + 2.0 * delta.astype(jnp.float32)).astype(jnp.bfloat16)


def local(
    tokens, key_projection_weight, adapter_down_factors, adapter_up_factors, request_adapter_index
):
    fits = (
        key_projection_weight.shape[0] % LANES == 0
        and tokens.shape[0] == LANES
        and adapter_down_factors.shape[0] == 1
        and HALVES * adapter_down_factors.shape[2] == LANES
        and lax.axis_size("pool") % (HALVES * CORES) == 0
        and lax.axis_size("rep") == 2
    )
    plan = split_depth if fits else route_rows
    return plan(
        tokens, key_projection_weight, adapter_down_factors, adapter_up_factors,
        request_adapter_index,
    )


def solution(mesh):
    in_specs = (
        P(("rep", "pool"), None),
        P("pool", None),
        P(("rep", "pool"), None, None),
        P(("rep", "pool"), None, None),
        P(("rep", "pool"), None),
    )
    out_specs = P(("rep", "pool"), None)
    return jax.shard_map(local, mesh=mesh, in_specs=in_specs, out_specs=out_specs, check_vma=False)
```

```python
import functools

import jax
import jax.numpy as jnp
from jax import lax
from jax.experimental import pallas as pl
from jax.experimental.pallas import tpu as pltpu
from jax.sharding import PartitionSpec as P

HALVES = 2
CORES = 2
W_FIRST = False
LANES = 128
MESH = pl.DeviceIdType.MESH


def kernel(
    group, reps, parts,
    x_hbm, w_hbm, a_hbm, b_hbm, id_ref, out_ref,
    xr, ar, wf, bp, idr, slots, acc, base, sp, srecv, s2, s2m, cpart, pair, cpair, crecv,
    x_send, x_recv, a_send, a_recv, w_send, w_recv, f_send, f_recv, b_send, b_recv,
    i_send, i_recv, s_send, s_recv, t_send, t_recv, p_send, p_recv, c_send, c_recv, local_sem,
):
    rep = lax.axis_index("rep")
    pool = lax.axis_index("pool")
    half, e = pool // group, pool % group
    rows, out_width = out_ref.shape
    depth = w_hbm.shape[0]
    low = group * depth
    rank = b_hbm.shape[0]
    devices = group * HALVES
    part = out_width // parts
    partner = (pool + group) % devices
    sides = group // CORES
    core = e % CORES
    core_peer = half * group + e + 1 - 2 * core

    def peer(k):
        return half * group + (e + k) % group

    def place(i):
        return (i % CORES) * sides + i // CORES

    def row_at(i, count=1):
        return pl.ds(pl.multiple_of(i * rows, rows), count * rows)

    def col_at(i, size):
        return pl.ds(pl.multiple_of(i * size, size), size)

    def depth_at(b, i):
        return pl.ds(pl.multiple_of(b * low + i * depth, depth), depth)

    def remote(src, dst, send, recv, device):
        return pltpu.make_async_remote_copy(
            src_ref=src, dst_ref=dst, send_sem=send, recv_sem=recv,
            device_id=device, device_id_type=MESH,
        )

    barrier = pltpu.get_barrier_semaphore()
    for k in range(1, devices):
        pl.semaphore_signal(
            barrier, inc=1, device_id={"pool": (pool + k) % devices}, device_id_type=MESH
        )
    for k in range(1, reps):
        pl.semaphore_signal(
            barrier, inc=1, device_id={"rep": (rep + k) % reps}, device_id_type=MESH
        )

    my_place = place(e)
    my_rows = row_at(my_place)
    slot = e * HALVES + half
    my_slot = pl.ds(pl.multiple_of(slot * rank, rank), rank)
    own_b = pl.ds(pl.multiple_of(half * rank, rank), rank)
    own = [
        pltpu.make_async_copy(w_hbm, wf.at[half], local_sem.at[0]),
        pltpu.make_async_copy(b_hbm, bp.at[own_b], local_sem.at[1]),
    ]
    for b in range(HALVES):
        own.append(pltpu.make_async_copy(
            x_hbm.at[:, depth_at(b, e)], xr.at[b, my_rows], local_sem.at[2 + 2 * b]
        ))
        own.append(pltpu.make_async_copy(
            a_hbm.at[:, depth_at(b, e)], ar.at[b, my_slot], local_sem.at[3 + 2 * b]
        ))
    for copy in own:
        copy.start()
    idr[my_place] = id_ref[...]
    pl.semaphore_wait(barrier, devices - 1 + reps - 1)

    sends, x_copies, a_copies = [], [], []

    def launch(copy):
        copy.start()
        sends.append(copy)
        return copy

    def send_a(n, device):
        for b in range(HALVES):
            a_copies.append(launch(remote(
                a_hbm.at[:, depth_at(b, device % group)], ar.at[b, my_slot],
                a_send.at[b, n], a_recv.at[b, n], {"pool": device},
            )))

    share = parts // reps
    w_copies = []

    def send_w():
        for n in range(share):
            at = col_at(n * reps + rep, part)
            w_copies.append(launch(remote(
                w_hbm.at[:, at], wf.at[half, :, at], w_send.at[n], w_recv.at[n],
                {"pool": partner},
            )))

    if W_FIRST:
        send_w()
    for k in range(1, group):
        x_copies.append(launch(remote(
            id_ref, idr.at[my_place], i_send.at[k], i_recv.at[k], {"pool": peer(k)}
        )))
    for k in range(1, group):
        for b in range(HALVES):
            x_copies.append(launch(remote(
                x_hbm.at[:, depth_at(b, (e + k) % group)], xr.at[b, my_rows],
                x_send.at[b, k], x_recv.at[b, k], {"pool": peer(k)},
            )))
        send_a(group + k, (1 - half) * group + (e + k) % group)
        send_a(k, peer(k))
    send_a(group, partner)
    if not W_FIRST:
        send_w()
    b_copy = launch(remote(b_hbm, bp.at[own_b], b_send, b_recv, {"pool": partner}))

    for copy in x_copies:
        copy.wait_recv()
    for copy in own:
        copy.wait()

    lane = lax.broadcasted_iota(jnp.int32, (rows, LANES), 1)
    eye = lane == lax.broadcasted_iota(jnp.int32, (rows, LANES), 0)
    upper = jnp.where(lane >= rank, 1.0, 0.0)

    @pl.loop(0, group)
    def _(i):
        line = jnp.broadcast_to(idr[i], (rows, LANES)).astype(jnp.float32)
        column = jnp.sum(jnp.where(eye, line, 0.0), axis=1, keepdims=True)
        column = jnp.where(
            column >= float(group), HALVES * (column - float(group)) + 1.0, HALVES * column
        )
        slots[row_at(i)] = jnp.broadcast_to(column, (rows, LANES)) - upper

    @pl.loop(0, parts)
    def _(j):
        at = col_at(j, part)
        base[:, at] = jnp.dot(
            xr[half], wf[half, :, at], preferred_element_type=jnp.float32
        )

    def forward_w():
        copies = []
        for n in range(share):
            w_copies[n].wait_recv()
            piece = wf.at[1 - half, :, col_at(n * reps + rep, part)]
            copies.append(launch(remote(
                piece, piece, f_send.at[n], f_recv.at[n], {"rep": (rep + 1) % reps}
            )))
        return copies

    if W_FIRST:
        f_copies = forward_w()
    for copy in a_copies:
        copy.wait_recv()
    acc[...] = jnp.zeros_like(acc)
    wide = 4 * rank

    @pl.loop(0, devices * rank // wide)
    def _(j):
        at = pl.ds(pl.multiple_of(j * wide, wide), wide)
        t = jnp.zeros((group * rows, wide), jnp.float32)
        for b in range(HALVES):
            t += lax.dot_general(
                xr[b], ar[b, at], (((1,), (1,)), ((), ())),
                preferred_element_type=jnp.float32,
            )
        first = (4 * j).astype(jnp.float32)
        acc[...] = jnp.where(
            slots[...] == first, t[:, :LANES],
            jnp.where(slots[...] == first + 2.0, t[:, LANES:], acc[...]),
        )

    sp[...] = acc[...].astype(jnp.bfloat16)
    s_copies = []
    for k in range(1, group):
        s_copies.append(launch(remote(
            sp.at[row_at(place((e + k) % group))], srecv.at[k], s_send.at[k], s_recv.at[k],
            {"pool": peer(k)},
        )))
    if not W_FIRST:
        f_copies = forward_w()
    total = acc[my_rows]
    for k in range(1, group):
        s_copies[k - 1].wait_recv()
        total += srecv[k].astype(jnp.float32)
    s2[my_rows] = total.astype(jnp.bfloat16)
    t_copies = []
    for k in range(1, group):
        t_copies.append(launch(remote(
            s2.at[my_rows], s2.at[my_rows], t_send.at[k], t_recv.at[k], {"pool": peer(k)}
        )))

    for n in range(share):
        f_copies[n].wait_recv()

    @pl.loop(0, parts)
    def _(j):
        at = col_at(j, part)
        base[:, at] += jnp.dot(
            xr[1 - half], wf[1 - half, :, at], preferred_element_type=jnp.float32
        )

    for copy in t_copies:
        copy.wait_recv()
    b_copy.wait_recv()
    mine = (HALVES * e).astype(jnp.float32)
    s2m[...] = jnp.where(
        slots[...] == mine, s2[...].astype(jnp.float32), 0.0
    ).astype(jnp.bfloat16)

    here, there = row_at(core * sides, sides), row_at((1 - core) * sides, sides)
    p_copies, c_copies = [], []

    def pair_up(j):
        at = pl.ds(j * part, part)
        update = jnp.dot(s2m[...], bp[:, at], preferred_element_type=jnp.float32)
        update = update.astype(jnp.bfloat16).astype(jnp.float32)
        base[:, at] += 2.0 * update
        cpart[:, at] = base[there, at].astype(jnp.bfloat16)
        p_copies.append(launch(remote(
            cpart.at[:, at], pair.at[:, at], p_send.at[j], p_recv.at[j], {"pool": core_peer}
        )))

    def hand_on(j):
        at = pl.ds(j * part, part)
        p_copies[j].wait_recv()
        cpair[:, at] = (base[here, at] + pair[:, at].astype(jnp.float32)).astype(jnp.bfloat16)
        for k in range(1, sides):
            to = (e // CORES + k) % sides
            c_copies.append(launch(remote(
                cpair.at[row_at(to), at], crecv.at[k, :, at], c_send.at[j, k], c_recv.at[j, k],
                {"pool": half * group + to * CORES + core},
            )))

    for j in range(parts):
        pair_up(j)
        if j > 0:
            hand_on(j - 1)
    hand_on(parts - 1)
    for j in range(parts):
        at = pl.ds(j * part, part)
        value = cpair[row_at(e // CORES), at].astype(jnp.float32)
        for k in range(1, sides):
            c_copies[j * (sides - 1) + k - 1].wait_recv()
            value += crecv[k, :, at].astype(jnp.float32)
        out_ref[:, at] = value.astype(jnp.bfloat16)
    for copy in sends:
        copy.wait_send()


def split_depth(
    tokens, key_projection_weight, adapter_down_factors, adapter_up_factors, request_adapter_index
):
    rows = tokens.shape[0]
    depth, out_width = key_projection_weight.shape
    rank = adapter_down_factors.shape[2]
    devices = lax.axis_size("pool")
    reps = lax.axis_size("rep")
    group = devices // HALVES
    sides = group // CORES
    parts = 2 * reps
    everyone = group * rows
    ids = request_adapter_index.reshape(1, rows)
    bf16, f32 = jnp.bfloat16, jnp.float32
    dma = pltpu.SemaphoreType.DMA
    hbm, vmem = pl.BlockSpec(memory_space=pl.ANY), pl.BlockSpec(memory_space=pltpu.VMEM)
    return pl.pallas_call(
        functools.partial(kernel, group, reps, parts),
        out_shape=jax.ShapeDtypeStruct((rows, out_width), bf16),
        in_specs=[hbm, hbm, hbm, hbm, vmem],
        out_specs=vmem,
        scratch_shapes=[
            pltpu.VMEM((HALVES, everyone, depth), bf16),
            pltpu.VMEM((HALVES, devices * rank, depth), bf16),
            pltpu.VMEM((HALVES, depth, out_width), bf16),
            pltpu.VMEM((HALVES * rank, out_width), bf16),
            pltpu.VMEM((group, 1, rows), jnp.int32),
            pltpu.VMEM((everyone, LANES), f32),
            pltpu.VMEM((everyone, LANES), f32),
            pltpu.VMEM((everyone, out_width), f32),
            pltpu.VMEM((everyone, LANES), bf16),
            pltpu.VMEM((group, rows, LANES), bf16),
            pltpu.VMEM((everyone, LANES), bf16),
            pltpu.VMEM((everyone, LANES), bf16),
            pltpu.VMEM((sides * rows, out_width), bf16),
            pltpu.VMEM((sides * rows, out_width), bf16),
            pltpu.VMEM((sides * rows, out_width), bf16),
            pltpu.VMEM((sides, rows, out_width), bf16),
            dma((HALVES, group)), dma((HALVES, group)),
            dma((HALVES, devices)), dma((HALVES, devices)),
            dma((parts,)), dma((parts,)),
            dma((parts,)), dma((parts,)),
            dma, dma,
            dma((group,)), dma((group,)),
            dma((group,)), dma((group,)),
            dma((group,)), dma((group,)),
            dma((parts,)), dma((parts,)),
            dma((parts, sides)), dma((parts, sides)),
            dma((6,)),
        ],
        compiler_params=pltpu.CompilerParams(
            collective_id=0, has_side_effects=True, vmem_limit_bytes=60 << 20
        ),
    )(
        tokens, key_projection_weight, jnp.swapaxes(adapter_down_factors, 1, 2)[0],
        adapter_up_factors[0], ids,
    )


def route_rows(
    tokens, key_projection_weight, adapter_down_factors, adapter_up_factors, request_adapter_index
):
    row_count = tokens.shape[0]
    width = tokens.shape[1]
    devices = lax.axis_size("pool")
    rows_by_device = adapter_down_factors.shape[0]
    out_width = key_projection_weight.shape[1]
    per_adapter = max(2, 2 * row_count // (rows_by_device * devices))
    capacity = rows_by_device * per_adapter
    adapter_col = request_adapter_index[:, 0]
    same = adapter_col[:, None] == adapter_col[None, :]
    positions = jnp.arange(row_count, dtype=jnp.int32)
    earlier = positions[None, :] < positions[:, None]
    rank_within = jnp.sum((same & earlier).astype(jnp.int32), axis=1)
    slot_index = adapter_col * per_adapter + rank_within
    base = jnp.dot(
        tokens,
        lax.all_gather(key_projection_weight, "pool", axis=0, tiled=True),
        preferred_element_type=jnp.float32,
    )
    outgoing = jnp.zeros((devices * capacity, width), jnp.bfloat16).at[slot_index].set(tokens)
    outgoing = outgoing.reshape(devices, capacity, width)
    received_rows = lax.all_to_all(outgoing, "pool", split_axis=0, concat_axis=0, tiled=True)
    received_rows = received_rows.reshape(devices, rows_by_device, per_adapter, width)
    rank_reduced = jnp.einsum(
        "qhey,hyt->qhet", received_rows, adapter_down_factors, preferred_element_type=jnp.float32
    ).astype(jnp.bfloat16)
    expanded = jnp.einsum(
        "zydk,ykj->zydj", rank_reduced, adapter_up_factors, preferred_element_type=jnp.float32
    ).astype(jnp.bfloat16)
    returned = lax.all_to_all(
        expanded.reshape(devices, capacity, out_width),
        "pool",
        split_axis=0,
        concat_axis=0,
        tiled=True,
    )
    delta = returned.reshape(devices * capacity, out_width)[slot_index]
    return (base + 2.0 * delta.astype(jnp.float32)).astype(jnp.bfloat16)


def local(
    tokens, key_projection_weight, adapter_down_factors, adapter_up_factors, request_adapter_index
):
    fits = (
        key_projection_weight.shape[0] % LANES == 0
        and tokens.shape[0] == LANES
        and adapter_down_factors.shape[0] == 1
        and HALVES * adapter_down_factors.shape[2] == LANES
        and lax.axis_size("pool") % (HALVES * CORES) == 0
        and lax.axis_size("rep") == 2
    )
    plan = split_depth if fits else route_rows
    return plan(
        tokens, key_projection_weight, adapter_down_factors, adapter_up_factors,
        request_adapter_index,
    )


def solution(mesh):
    in_specs = (
        P(("rep", "pool"), None),
        P("pool", None),
        P(("rep", "pool"), None, None),
        P(("rep", "pool"), None, None),
        P(("rep", "pool"), None),
    )
    out_specs = P(("rep", "pool"), None)
    return jax.shard_map(local, mesh=mesh, in_specs=in_specs, out_specs=out_specs, check_vma=False)
```
